256 devices in a mesh: layer: 16 (over z, core), row: 4 (over x), col: 4 (over y).
Axes of the slice: x: 4, y: 4, z: 8, core: 2. Of those that a mesh axis runs over, the one named last changes fastest.
Arguments:
- lower_panels: bfloat16 [48, 5120, 2048], P('layer', 'row', 'col'), may hold values from -4 to 4
- upper_panels: bfloat16 [48, 5120, 2048], P('layer', 'col', 'row'), may hold values from -0.125 to 0.125
- lower_lists: int32 [16, 2], P('layer'), may hold values from 0 to 2
- upper_lists: int32 [16, 2], P('layer'), may hold values from 0 to 2
- block_counts: int32 [16], P('layer'), may hold values from 1 to 2, as said below
- ancestor: bfloat16 [320, 16, 5120], P('row', 'layer', 'col'), may hold values from -6 to 6
- pivot_inverse: float32 [320, 16], P('row', 'layer'), may hold values from 0.3 to 3
Outputs:
- updated: float32 [320, 16, 5120], P('row', 'layer', 'col')
The draws below stay inside these ranges and needn't reach their ends.
Inputs may be any that keep to these rules, and one draw needn't show every extreme that they name: `block_counts`: each layer lists at least one pair; some layer lists exactly 2 and some layer exactly one. `lower_lists`: entries at slots from a layer's count onward are ignored. `upper_lists`: entries at slots from a layer's count onward are ignored.
All inputs are finite; a program needn't handle non-finite values.
Results may differ from the reference program's by a relative error of at most 0.0003.
Values may be sent and summed in bfloat16 or wider, within the bound.
A program may use at most 128 MiB of HBM per device.

```python
import math
import jax
import jax.numpy as jnp
from jax import lax

ORDER = 5120
TILE = 2048
POOL = 3
LISTED = 2
LAYERS = 16
ROW_GROUPS = 320


def draw_block_counts(key, part):
    values = jax.random.randint(key, (LAYERS,), 1, LISTED + 1).astype(jnp.int32)
    position = jax.random.randint(jax.random.fold_in(key, 7), (), 0, LAYERS).astype(jnp.int32)
    following = ((position + 1) % LAYERS).astype(jnp.int32)
    values = values.at[position].set(LISTED)
    values = values.at[following].set(1)
    return values.astype(jnp.int32)


def with_ends(result, own_key, least, largest):
    shape = result.shape
    place = [jax.random.randint(jax.random.fold_in(own_key, axis), (), 0, shape[axis]) for axis in range(len(shape))]
    result = result.at[tuple(place)].set(least)
    longest = shape.index(max(shape))
    place[longest] = (place[longest] + 1) % shape[longest]
    return result.at[tuple(place)].set(largest)


def levels(key, dims, split, low, largest):
    gain, own = 1.0, jax.random.fold_in(key, 6)
    for axis_at, parts in split:
        draws = jnp.exp(jax.random.uniform(jax.random.fold_in(own, axis_at), (parts,), jnp.float32, low / len(split), largest / len(split)))
        gain = gain * jnp.repeat(draws, dims[axis_at] // parts).reshape([-1 if axis == axis_at else 1 for axis in range(len(dims))])
    return gain


def normal_values(own_key, shape, spread, bound, split=(), kind=jnp.bfloat16):
    result = spread * jax.random.normal(own_key, shape, jnp.float32)
    if split:
        result = result * levels(own_key, shape, split, -0.22, 0.18)
    return jnp.clip(result, -bound, bound).astype(kind)


def setup_inputs(seed: int = 0) -> dict:
    splits = jax.random.split(jax.random.key(seed), 8)
    return {
        "lower_panels": normal_values(splits[0], (LAYERS * POOL, ORDER, TILE), 0.25, 4.0, ((0, 16), (1, 4), (2, 4))),
        "upper_panels": normal_values(splits[1], (LAYERS * POOL, ORDER, TILE), TILE ** -0.5, 0.125, ((0, 16), (1, 4), (2, 4))),
        "lower_lists": with_ends(jax.random.randint(splits[2], (LAYERS, LISTED), 0, POOL), jax.random.fold_in(splits[2], 1), 0, POOL - 1).astype(jnp.int32),
        "upper_lists": with_ends(jax.random.randint(splits[3], (LAYERS, LISTED), 0, POOL), jax.random.fold_in(splits[3], 1), 0, POOL - 1).astype(jnp.int32),
        "block_counts": draw_block_counts(jax.random.fold_in(splits[7], 71), 0),
        "ancestor": normal_values(splits[5], (ROW_GROUPS, LAYERS, ORDER), 1.0, 6.0, ((0, 4), (1, 16), (2, 4))),
        "pivot_inverse": jnp.clip(jnp.exp(math.log(3.0) - 2.3025851 * jax.random.uniform(splits[6], (ROW_GROUPS, LAYERS), jnp.float32) ** levels(splits[6], (ROW_GROUPS, LAYERS), ((0, 4), (1, 16)), -0.2, 0.2)), 0.3, 3.0),
    }


def reference(lower_panels, upper_panels, lower_lists, upper_lists, block_counts, ancestor, pivot_inverse):
    def layer_step(total, layer):
        for slot in range(LISTED):
            lower_index = (layer * POOL + lower_lists[layer, slot]).astype(jnp.int32)
            upper_index = (layer * POOL + upper_lists[layer, slot]).astype(jnp.int32)
            lower_one = lax.dynamic_index_in_dim(lower_panels, lower_index, 0, keepdims=False)
            upper_one = lax.dynamic_index_in_dim(upper_panels, upper_index, 0, keepdims=False)

            def add_pair(running):
                return running + jnp.dot(lower_one, upper_one.T, preferred_element_type=jnp.float32)

            def keep_same(running):
                return running

            total = lax.cond(slot < block_counts[layer], add_pair, keep_same, total)
        return total, None

    start_total = jnp.zeros((ORDER, ORDER), jnp.float32)
    total, ignored = lax.scan(layer_step, start_total, jnp.arange(LAYERS, dtype=jnp.int32))
    grouped = total.reshape(ROW_GROUPS, LAYERS, ORDER)
    return (ancestor.astype(jnp.float32) - grouped) * pivot_inverse[:, :, None]
```

```python
import jax
import jax.numpy as jnp
from jax import lax
from jax.experimental import pallas as pl
from jax.experimental.pallas import tpu as pltpu
from jax.sharding import PartitionSpec as P

MESH = pl.DeviceIdType.MESH
GROUP = 128
CHUNKS = (128, 128, 256, 256, 256, 128, 128)
DIRECT = (0, 0, 0, 0, 0, 1, 1)
AHEAD = 2
NT = (((1,), (1,)), ((), ()))


def kernel(
    lower_list, upper_list, count, lower_hbm, upper_hbm, ancestor, pivots, out,
    first_lower, first_upper, rest_lower, rest_upper, lower_all, upper_all, product, from_core, from_z,
    load_sem, own_send, own_recv, fwd_send, fwd_recv, core_send, core_recv, z_send, z_recv,
):
    layer, x, y = lax.axis_index("layer"), lax.axis_index("row"), lax.axis_index("col")
    z, core = lax.div(layer, 2), lax.rem(layer, 2)
    sign = 1 - 2 * core
    starts = [sum(CHUNKS[:i]) for i in range(len(CHUNKS))]
    last = len(CHUNKS) - 1
    first = CHUNKS[0]
    total_rows = lower_hbm.shape[1]

    loads = []
    for i, (hbm, head, rest) in enumerate(
        ((lower_hbm, first_lower, rest_lower), (upper_hbm, first_upper, rest_upper))
    ):
        loads.append(pltpu.make_async_copy(hbm.at[:, pl.ds(0, first)], head, load_sem.at[i, 0]))
        loads.append(
            pltpu.make_async_copy(hbm.at[:, pl.ds(first, total_rows - first)], rest, load_sem.at[i, 1])
        )
    for i in (0, 2, 1, 3):
        loads[i].start()

    def at_z(distance):
        return {"layer": lax.rem(layer + 2 * distance + 32, 16)}

    def at_ring(axis, step):
        return {"col": lax.rem(y + step + 4, 4)} if axis == 0 else {"row": lax.rem(x + step + 4, 4)}

    barrier = pltpu.get_barrier_semaphore()
    met = [at_ring(a, s) for a in (0, 1) for s in (1, -1)] + [{"layer": layer + sign}]
    met += [at_z(d) for d in range(1, 8)]
    for target in met:
        pl.semaphore_signal(barrier, inc=1, device_id=target, device_id_type=MESH)

    position = lax.broadcasted_iota(jnp.int32, (GROUP, GROUP), 0)
    source = lax.broadcasted_iota(jnp.int32, (GROUP, GROUP), 1)
    wanted = (position % 8) * 16 + ((position // 8) % 8) * 2 + position // 64
    place = jnp.where(wanted == source, 1.0, 0.0).astype(jnp.bfloat16)
    buffers = (lower_all, upper_all)
    mine = (y, x)

    def prepare(i):
        low, up = (first_lower, first_upper) if i == 0 else (rest_lower, rest_upper)
        offset = 0 if i == 0 else first
        for slot in range(2):
            live = slot < count[0]
            lo, uo = lower_list[0, slot], upper_list[0, slot]
            for g in range(CHUNKS[i] // GROUP):
                row = starts[i] + g * GROUP
                rows = pl.ds(row - offset, GROUP)
                moved = jnp.dot(place, low[lo, rows, :], preferred_element_type=jnp.float32)
                moved = jnp.where(live, moved, 0.0)
                lower_all[y, slot, pl.ds(row, GROUP), :] = moved.astype(jnp.bfloat16)
                upper_all[x, slot, pl.ds(row, GROUP), :] = up[uo, rows, :]

    def own(axis, way, i, origin):
        step = 1 - 2 * way
        part = buffers[axis].at[origin, :, pl.ds(starts[i], CHUNKS[i]), :]
        return pltpu.make_async_remote_copy(
            part, part, own_send.at[axis, way, i], own_recv.at[axis, way, i],
            device_id=at_ring(axis, step), device_id_type=MESH,
        )

    def fwd(axis, way, i, origin):
        step = 1 - 2 * way
        part = buffers[axis].at[origin, way, pl.ds(starts[i], CHUNKS[i]), :]
        return pltpu.make_async_remote_copy(
            part, part, fwd_send.at[axis, way, i], fwd_recv.at[axis, way, i],
            device_id=at_ring(axis, step), device_id_type=MESH,
        )

    links = [(axis, way) for way in (0, 1) for axis in (0, 1)]

    def send_own(i):
        for axis, way in links:
            own(axis, way, i, mine[axis]).start()

    def pass_on(i):
        for axis, way in links:
            origin = lax.rem(mine[axis] - (1 - 2 * way) + 4, 4)
            own(axis, way, i, origin).wait_recv()
            fwd(axis, way, i, origin).start()

    def wait_far(i):
        for axis, way in links:
            fwd(axis, way, i, lax.rem(mine[axis] + 2, 4)).wait_recv()

    def block(row, rows, col, cols):
        total = None
        for j in range(4):
            for slot in range(2):
                term = lax.dot_general(
                    lower_all[j, slot, pl.ds(row, rows), :], upper_all[j, slot, pl.ds(col, cols), :],
                    NT, preferred_element_type=jnp.float32,
                )
                total = term if total is None else total + term
        for g in range(rows // GROUP):
            where = row // 16 + g * 8
            if not isinstance(where, int):
                where = pl.multiple_of(where, 8)
            product[:, :, pl.ds(where, 8), pl.ds(col, cols)] = total[g * GROUP : (g + 1) * GROUP].reshape(
                2, 8, 8, cols
            )

    def down(i):
        end, col, cols = starts[i] + CHUNKS[i], starts[i], CHUNKS[i]
        if end >= 256:

            @pl.loop(0, end // 256)
            def _(t):
                block(pl.multiple_of(t * 256, 256), 256, col, cols)

        if end % 256:
            block(end // 256 * 256, end % 256, col, cols)

    def across(i):
        row, rows, end = starts[i], CHUNKS[i], starts[i]
        if end >= 256:

            @pl.loop(0, end // 256)
            def _(t):
                block(row, rows, pl.multiple_of(t * 256, 256), 256)

        if end % 256:
            block(row, rows, end // 256 * 256, end % 256)

    def rect(i, k):
        begin, end = starts[i], starts[i] + CHUNKS[i]
        if k == 0:
            return pl.ds(0, end // 16), pl.ds(begin, end - begin)
        return pl.ds(begin // 16, (end - begin) // 16), pl.ds(0, begin)

    def to_core(i, k):
        rows, cols = rect(i, k)
        return pltpu.make_async_remote_copy(
            product.at[1 - core, :, rows, cols], from_core.at[:, rows, cols],
            core_send.at[i, k], core_recv.at[i, k],
            device_id={"layer": layer + sign}, device_id_type=MESH,
        )

    def to_z(i, k, slot, target, hop):
        rows, cols = rect(i, k)
        return pltpu.make_async_remote_copy(
            product.at[core, lax.rem(z + target + 16, 8), rows, cols], from_z.at[slot, rows, cols],
            z_send.at[i, k, slot], z_recv.at[i, k, slot],
            device_id=at_z(hop), device_id_type=MESH,
        )

    def parts(i):
        return (0, 1) if i else (0,)

    def add_core(i, k):
        to_core(i, k).wait_recv()
        rows, cols = rect(i, k)

        @pl.loop(0, 8)
        def _(t):
            product[core, t, rows, cols] = product[core, t, rows, cols] + from_core[t, rows, cols]

    def add_z(i, k, slot, target):
        rows, cols = rect(i, k)
        at = lax.rem(z + target + 16, 8)
        product[core, at, rows, cols] = product[core, at, rows, cols] + from_z[slot, rows, cols]

    def advance(i, step):
        for k in parts(i):
            if step == 0:
                add_core(i, k)
            if DIRECT[i]:
                for d in (4, 3, 5, 2, 6, 1, 7):
                    if step == 0:
                        to_z(i, k, d - 1, d, d).start()
                    else:
                        to_z(i, k, d - 1, d, d).wait_recv()
                        add_z(i, k, d - 1, 0)
                continue
            if step:
                to_z(i, k, step - 1, 0, sign).wait_recv()
                add_z(i, k, step - 1, sign * (4 - step))
            if step < 4:
                to_z(i, k, step, sign * (4 - step), sign).start()
            if 0 < step < 4:
                to_z(i, k, 3 + step, 0, -sign).wait_recv()
                add_z(i, k, 3 + step, -sign * (3 - step))
            if step < 3:
                to_z(i, k, 4 + step, -sign * (3 - step), -sign).start()

    def steps(i):
        return 2 if DIRECT[i] else 5

    pending = []

    def advance_all(count):
        for _ in range(count):
            for entry in list(pending):
                advance(entry[0], entry[1])
                entry[1] += 1
                if entry[1] == steps(entry[0]):
                    pending.remove(entry)

    def finish(i):
        wait_far(i)
        down(i)
        to_core(i, 0).start()
        if i:
            across(i)
            to_core(i, 1).start()

    loads[0].wait()
    loads[2].wait()
    prepare(0)
    pl.semaphore_wait(barrier, len(met))
    send_own(0)
    loads[1].wait()
    loads[3].wait()
    for i in range(1, AHEAD):
        prepare(i)
        send_own(i)
    for i in range(last + 1):
        if i + AHEAD <= last:
            prepare(i + AHEAD)
            send_own(i + AHEAD)
        pass_on(i)
        if i:
            finish(i - 1)
            advance_all(1)
            pending.append([i - 1, 0])
    finish(last)
    pending.append([last, 0])
    advance_all(5)

    @pl.loop(0, total_rows // 256)
    def _(t):
        rows = pl.ds(pl.multiple_of(t * 16, 16), 16)
        rest = ancestor[rows, :].astype(jnp.float32) - product[core, z, rows, :]
        out[rows, :] = rest * pivots[rows, :]

    for i in range(last + 1):
        for axis, way in links:
            own(axis, way, i, mine[axis]).wait_send()
            fwd(axis, way, i, lax.rem(mine[axis] - (1 - 2 * way) + 4, 4)).wait_send()
        for k in parts(i):
            to_core(i, k).wait_send()
            for slot in range(7):
                if DIRECT[i]:
                    to_z(i, k, slot, slot + 1, slot + 1).wait_send()
                elif slot < 4:
                    to_z(i, k, slot, sign * (4 - slot), sign).wait_send()
                else:
                    to_z(i, k, slot, -sign * (7 - slot), -sign).wait_send()


def per_device(
    lower_panels, upper_panels, lower_lists, upper_lists, block_counts, ancestor, pivot_inverse
):
    pool, rows, width = lower_panels.shape
    groups, _, cols = ancestor.shape
    chunks = len(CHUNKS)
    smem = pl.BlockSpec(memory_space=pltpu.SMEM)
    vmem = pl.BlockSpec(memory_space=pltpu.VMEM)
    hbm = pl.BlockSpec(memory_space=pl.ANY)
    dma = pltpu.SemaphoreType.DMA
    updated = pl.pallas_call(
        kernel,
        out_shape=jax.ShapeDtypeStruct((groups, cols), jnp.float32),
        in_specs=[smem, smem, smem, hbm, hbm, vmem, vmem],
        out_specs=vmem,
        scratch_shapes=[
            pltpu.VMEM((pool, CHUNKS[0], width), jnp.bfloat16),
            pltpu.VMEM((pool, CHUNKS[0], width), jnp.bfloat16),
            pltpu.VMEM((pool, rows - CHUNKS[0], width), jnp.bfloat16),
            pltpu.VMEM((pool, rows - CHUNKS[0], width), jnp.bfloat16),
            pltpu.VMEM((4, 2, rows, width), jnp.bfloat16),
            pltpu.VMEM((4, 2, cols, width), jnp.bfloat16),
            pltpu.VMEM((2, 8, groups, cols), jnp.float32),
            pltpu.VMEM((8, groups, cols), jnp.float32),
            pltpu.VMEM((7, groups, cols), jnp.float32),
            dma((2, 2)),
            dma((2, 2, chunks)),
            dma((2, 2, chunks)),
            dma((2, 2, chunks)),
            dma((2, 2, chunks)),
            dma((chunks, 2)),
            dma((chunks, 2)),
            dma((chunks, 2, 7)),
            dma((chunks, 2, 7)),
        ],
        compiler_params=pltpu.CompilerParams(
            collective_id=0, has_side_effects=True, vmem_limit_bytes=58 * 2**20
        ),
        cost_estimate=pl.CostEstimate(
            flops=4 * rows * cols * width * 4, bytes_accessed=9 * 2**20, transcendentals=0
        ),
    )(
        lower_lists, upper_lists, block_counts, lower_panels, upper_panels,
        ancestor.reshape(groups, cols), pivot_inverse,
    )
    return updated.reshape(groups, 1, cols)


def solution(mesh):
    in_specs = (
        P("layer", "row", "col"),
        P("layer", "col", "row"),
        P("layer", None),
        P("layer", None),
        P("layer"),
        P("row", "layer", "col"),
        P("row", "layer"),
    )
    return jax.shard_map(
        per_device, mesh=mesh, in_specs=in_specs, out_specs=P("row", "layer", "col"), check_vma=False
    )
```

```python
import jax
import jax.numpy as jnp
from jax import lax
from jax.experimental import pallas as pl
from jax.experimental.pallas import tpu as pltpu
from jax.sharding import PartitionSpec as P

MESH = pl.DeviceIdType.MESH
GROUP = 128
CHUNKS = (256,) * 5
STRIPS = (1,) * 5
SPLIT = (0, 0, 0, 0, 1)
AHEAD = 1
STEPS = 5
NT = (((1,), (1,)), ((), ()))


def kernel(
    lower_list, upper_list, count, lower_hbm, upper_hbm, out,
    first_lower, first_upper, rest_lower, rest_upper, lower_all, upper_all, product, from_core, from_z,
    load_sem, own_send, own_recv, fwd_send, fwd_recv, core_send, core_recv, z_send, z_recv,
):
    layer, x, y = lax.axis_index("layer"), lax.axis_index("row"), lax.axis_index("col")
    z, core = lax.div(layer, 2), lax.rem(layer, 2)
    sign = 1 - 2 * core
    starts = [sum(CHUNKS[:i]) for i in range(len(CHUNKS))]
    last = len(CHUNKS) - 1
    ends = [sum(STRIPS[: s + 1]) for s in range(len(STRIPS))]
    edges = [0] + [sum(CHUNKS[:e]) for e in ends]
    first = CHUNKS[0]
    total_rows = lower_hbm.shape[1]

    loads = []
    for i, (hbm, head, rest) in enumerate(
        ((lower_hbm, first_lower, rest_lower), (upper_hbm, first_upper, rest_upper))
    ):
        loads.append(pltpu.make_async_copy(hbm.at[:, pl.ds(0, first)], head, load_sem.at[i, 0]))
        loads.append(
            pltpu.make_async_copy(hbm.at[:, pl.ds(first, total_rows - first)], rest, load_sem.at[i, 1])
        )
    for i in (0, 2, 1, 3):
        loads[i].start()

    def at_z(distance):
        return {"layer": lax.rem(layer + 2 * distance + 32, 16)}

    def at_ring(axis, step):
        return {"col": lax.rem(y + step + 4, 4)} if axis == 0 else {"row": lax.rem(x + step + 4, 4)}

    barrier = pltpu.get_barrier_semaphore()
    met = [at_ring(a, s) for a in (0, 1) for s in (1, -1)] + [{"layer": layer + sign}]
    met += [at_z(d) for d in (1, -1)]
    for target in met:
        pl.semaphore_signal(barrier, inc=1, device_id=target, device_id_type=MESH)

    position = lax.broadcasted_iota(jnp.int32, (GROUP, GROUP), 0)
    source = lax.broadcasted_iota(jnp.int32, (GROUP, GROUP), 1)
    wanted = (position % 8) * 16 + ((position // 8) % 8) * 2 + position // 64
    place = jnp.where(wanted == source, 1.0, 0.0).astype(jnp.bfloat16)
    buffers = (lower_all, upper_all)
    mine = (y, x)

    def prepare(i):
        low, up = (first_lower, first_upper) if i == 0 else (rest_lower, rest_upper)
        offset = 0 if i == 0 else first
        for slot in range(2):
            live = slot < count[0]
            lo, uo = lower_list[0, slot], upper_list[0, slot]
            for g in range(CHUNKS[i] // GROUP):
                row = starts[i] + g * GROUP
                rows = pl.ds(row - offset, GROUP)
                moved = jnp.dot(place, low[lo, rows, :], preferred_element_type=jnp.float32)
                moved = jnp.where(live, moved, 0.0)
                lower_all[y, slot, pl.ds(row, GROUP), :] = moved.astype(jnp.bfloat16)
                upper_all[x, slot, pl.ds(row, GROUP), :] = up[uo, rows, :]

    def own(axis, way, i, origin):
        step = 1 - 2 * way
        part = buffers[axis].at[origin, :, pl.ds(starts[i], CHUNKS[i]), :]
        return pltpu.make_async_remote_copy(
            part, part, own_send.at[axis, way, i], own_recv.at[axis, way, i],
            device_id=at_ring(axis, step), device_id_type=MESH,
        )

    def fwd(axis, way, i, origin):
        step = 1 - 2 * way
        part = buffers[axis].at[origin, way, pl.ds(starts[i], CHUNKS[i]), :]
        return pltpu.make_async_remote_copy(
            part, part, fwd_send.at[axis, way, i], fwd_recv.at[axis, way, i],
            device_id=at_ring(axis, step), device_id_type=MESH,
        )

    links = [(axis, way) for way in (0, 1) for axis in (0, 1)]

    def send_own(i):
        for axis, way in links:
            own(axis, way, i, mine[axis]).start()

    def pass_on(i):
        for axis, way in links:
            origin = lax.rem(mine[axis] - (1 - 2 * way) + 4, 4)
            own(axis, way, i, origin).wait_recv()
            fwd(axis, way, i, origin).start()

    def wait_far(i):
        for axis, way in links:
            fwd(axis, way, i, lax.rem(mine[axis] + 2, 4)).wait_recv()

    far = lax.rem(y + 2, 4)
    apart = lax.rem(x - y + 4, 4)
    half = lax.div(apart, 2)
    near_js = (lax.rem(far + 2 - half, 4), lax.rem(far + 3 - lax.div(apart, 3), 4))
    far_js = (far, lax.rem(far + jnp.maximum(apart, 1), 4))
    all_js = (0, 1, 2, 3)

    def block(row, rows, col, cols, js, more, keep):
        total = None
        for j in js:
            for slot in range(2):
                term = lax.dot_general(
                    lower_all[j, slot, pl.ds(row, rows), :], upper_all[j, slot, pl.ds(col, cols), :],
                    NT, preferred_element_type=jnp.float32,
                )
                total = term if total is None else total + term
        into, row0, col0 = keep
        for g in range(rows // GROUP):
            at = (slice(None), slice(None), pl.ds((row - row0) // 16 + g * 8, 8), pl.ds(col - col0, cols))
            piece = total[g * GROUP : (g + 1) * GROUP].reshape(2, 8, 8, cols)
            into[at] = into[at] + piece if more else piece

    def cut(end):
        return [(r, min(256, end - r)) for r in range(0, end, 256)]

    def multiply(i, js, more, done):
        begin, end = edges[i], edges[i + 1]
        for row, rows in cut(end):
            block(row, rows, begin, end - begin, js, more, (product[i][0], 0, begin))
        if done:
            to_core(i, 0).start()
            pending.append([i, 0, 0])
        for col, cols in cut(begin):
            block(begin, end - begin, col, cols, js, more, (product[i][1], begin, 0))
        if done and i:
            to_core(i, 1).start()
            pending.append([i, 1, 0])

    def rect(i, k):
        begin, end = edges[i], edges[i + 1]
        if k == 0:
            return pl.ds(0, end // 16), pl.ds(begin, end - begin)
        return pl.ds(begin // 16, (end - begin) // 16), pl.ds(0, begin)

    def to_core(i, k):
        return pltpu.make_async_remote_copy(
            product[i][k].at[1 - core], from_core[i][k],
            core_send.at[i, k], core_recv.at[i, k],
            device_id={"layer": layer + sign}, device_id_type=MESH,
        )

    def to_z(i, k, slot, target, hop):
        return pltpu.make_async_remote_copy(
            product[i][k].at[core, lax.rem(z + target + 16, 8)], from_z[i][k].at[slot],
            z_send.at[i, k, slot], z_recv.at[i, k, slot],
            device_id=at_z(hop), device_id_type=MESH,
        )

    def parts(i):
        return (0, 1) if i else (0,)

    def add_core(i, k):
        to_core(i, k).wait_recv()

        @pl.loop(0, 8)
        def _(t):
            product[i][k][core, t] = product[i][k][core, t] + from_core[i][k][t]

    def add_z(i, k, slot, target):
        at = lax.rem(z + target + 16, 8)
        product[i][k][core, at] = product[i][k][core, at] + from_z[i][k][slot]

    def advance(i, k, step):
        if step == 0:
            add_core(i, k)
        if step:
            to_z(i, k, step - 1, 0, sign).wait_recv()
            add_z(i, k, step - 1, sign * (4 - step))
        if step < 4:
            to_z(i, k, step, sign * (4 - step), sign).start()
        if 0 < step < 4:
            to_z(i, k, 3 + step, 0, -sign).wait_recv()
            add_z(i, k, 3 + step, -sign * (3 - step))
        if step < 3:
            to_z(i, k, 4 + step, -sign * (3 - step), -sign).start()

    pending = []

    def tick():
        for entry in list(pending):
            advance(*entry)
            entry[2] += 1
            if entry[2] == STEPS:
                pending.remove(entry)

    loads[0].wait()
    loads[2].wait()
    prepare(0)
    pl.semaphore_wait(barrier, len(met))
    send_own(0)
    loads[1].wait()
    loads[3].wait()
    for i in range(1, AHEAD):
        prepare(i)
        send_own(i)
    for i in range(last + 1):
        if i + AHEAD <= last:
            prepare(i + AHEAD)
            send_own(i + AHEAD)
        pass_on(i)
        tick()
        near = [s for s, end in enumerate(ends) if end == i + 1 and SPLIT[s]]
        for strip in near:
            multiply(strip, near_js, False, False)
        if i:
            wait_far(i - 1)
            tick()
        for strip, end in enumerate(ends):
            if end == i:
                multiply(strip, far_js if SPLIT[strip] else all_js, SPLIT[strip], True)
    wait_far(last)
    tick()
    multiply(len(STRIPS) - 1, far_js if SPLIT[-1] else all_js, SPLIT[-1], True)
    while pending:
        tick()

    for i in range(len(STRIPS)):
        for k in parts(i):
            rows, cols = rect(i, k)
            out[rows, cols] = product[i][k][core, z]

    for i in range(last + 1):
        for axis, way in links:
            own(axis, way, i, mine[axis]).wait_send()
            fwd(axis, way, i, lax.rem(mine[axis] - (1 - 2 * way) + 4, 4)).wait_send()
    for i in range(len(STRIPS)):
        for k in parts(i):
            to_core(i, k).wait_send()
            for slot in range(7):
                if slot < 4:
                    to_z(i, k, slot, sign * (4 - slot), sign).wait_send()
                else:
                    to_z(i, k, slot, -sign * (7 - slot), -sign).wait_send()


def per_device(
    lower_panels, upper_panels, lower_lists, upper_lists, block_counts, ancestor, pivot_inverse
):
    pool, rows, width = lower_panels.shape
    groups, _, cols = ancestor.shape
    chunks, strips = len(CHUNKS), len(STRIPS)
    smem = pl.BlockSpec(memory_space=pltpu.SMEM)
    vmem = pl.BlockSpec(memory_space=pltpu.VMEM)
    hbm = pl.BlockSpec(memory_space=pl.ANY)
    dma = pltpu.SemaphoreType.DMA

    def pieces(lead):
        shapes, begin = [], 0
        for i, count in enumerate(STRIPS):
            end = begin + sum(CHUNKS[sum(STRIPS[:i]) : sum(STRIPS[: i + 1])])
            down = pltpu.VMEM((*lead, end // 16, end - begin), jnp.float32)
            across = pltpu.VMEM((*lead, (end - begin) // 16, max(begin, 128)), jnp.float32)
            shapes.append((down, across) if begin else (down,))
            begin = end
        return tuple(shapes)

    total = pl.pallas_call(
        kernel,
        out_shape=jax.ShapeDtypeStruct((groups, cols), jnp.float32),
        in_specs=[smem, smem, smem, hbm, hbm],
        out_specs=vmem,
        scratch_shapes=[
            pltpu.VMEM((pool, CHUNKS[0], width), jnp.bfloat16),
            pltpu.VMEM((pool, CHUNKS[0], width), jnp.bfloat16),
            pltpu.VMEM((pool, rows - CHUNKS[0], width), jnp.bfloat16),
            pltpu.VMEM((pool, rows - CHUNKS[0], width), jnp.bfloat16),
            pltpu.VMEM((4, 2, rows, width), jnp.bfloat16),
            pltpu.VMEM((4, 2, cols, width), jnp.bfloat16),
            pieces((2, 8)),
            pieces((8,)),
            pieces((7,)),
            dma((2, 2)),
            dma((2, 2, chunks)),
            dma((2, 2, chunks)),
            dma((2, 2, chunks)),
            dma((2, 2, chunks)),
            dma((strips, 2)),
            dma((strips, 2)),
            dma((strips, 2, 7)),
            dma((strips, 2, 7)),
        ],
        compiler_params=pltpu.CompilerParams(
            collective_id=0, has_side_effects=True, vmem_limit_bytes=58 * 2**20
        ),
        cost_estimate=pl.CostEstimate(
            flops=4 * rows * cols * width * 4, bytes_accessed=9 * 2**20, transcendentals=0
        ),
    )(
        lower_lists, upper_lists, block_counts, lower_panels, upper_panels,
    )
    return (ancestor.astype(jnp.float32) - total.reshape(groups, 1, cols)) * pivot_inverse[:, :, None]


def solution(mesh):
    in_specs = (
        P("layer", "row", "col"),
        P("layer", "col", "row"),
        P("layer", None),
        P("layer", None),
        P("layer"),
        P("row", "layer", "col"),
        P("row", "layer"),
    )
    return jax.shard_map(
        per_device, mesh=mesh, in_specs=in_specs, out_specs=P("row", "layer", "col"), check_vma=False
    )
```

```python
import jax
import jax.numpy as jnp
from jax import lax
from jax.experimental import pallas as pl
from jax.experimental.pallas import tpu as pltpu
from jax.sharding import PartitionSpec as P

MESH = pl.DeviceIdType.MESH
GROUP = 128
CHUNKS = (256,) * 5
STRIPS = (1,) * 5
SPLIT = (0, 0, 0, 0, 1)
AHEAD = 1
STEPS = 5
NT = (((1,), (1,)), ((), ()))


def kernel(
    lower_list, upper_list, count, lower_hbm, upper_hbm, out,
    first_lower, first_upper, rest_lower, rest_upper, lower_all, upper_all, product, from_core, from_z,
    load_sem, own_send, own_recv, fwd_send, fwd_recv, core_send, core_recv, z_send, z_recv,
):
    layer, x, y = lax.axis_index("layer"), lax.axis_index("row"), lax.axis_index("col")
    z, core = lax.div(layer, 2), lax.rem(layer, 2)
    sign = 1 - 2 * core
    starts = [sum(CHUNKS[:i]) for i in range(len(CHUNKS))]
    last = len(CHUNKS) - 1
    ends = [sum(STRIPS[: s + 1]) for s in range(len(STRIPS))]
    edges = [0] + [sum(CHUNKS[:e]) for e in ends]
    first = CHUNKS[0]
    total_rows = lower_hbm.shape[1]

    loads = []
    for i, (hbm, head, rest) in enumerate(
        ((lower_hbm, first_lower, rest_lower), (upper_hbm, first_upper, rest_upper))
    ):
        loads.append(pltpu.make_async_copy(hbm.at[:, pl.ds(0, first)], head, load_sem.at[i, 0]))
        loads.append(
            pltpu.make_async_copy(hbm.at[:, pl.ds(first, total_rows - first)], rest, load_sem.at[i, 1])
        )
    for i in (0, 2, 1, 3):
        loads[i].start()

    def at_z(distance):
        return {"layer": lax.rem(layer + 2 * distance + 32, 16)}

    def at_ring(axis, step):
        return {"col": lax.rem(y + step + 4, 4)} if axis == 0 else {"row": lax.rem(x + step + 4, 4)}

    barrier = pltpu.get_barrier_semaphore()
    met = [at_ring(a, s) for a in (0, 1) for s in (1, -1)] + [{"layer": layer + sign}]
    met += [at_z(d) for d in (1, -1)]
    for target in met:
        pl.semaphore_signal(barrier, inc=1, device_id=target, device_id_type=MESH)

    position = lax.broadcasted_iota(jnp.int32, (GROUP, GROUP), 0)
    source = lax.broadcasted_iota(jnp.int32, (GROUP, GROUP), 1)
    wanted = (position % 8) * 16 + ((position // 8) % 8) * 2 + position // 64
    place = jnp.where(wanted == source, 1.0, 0.0).astype(jnp.bfloat16)
    buffers = (lower_all, upper_all)
    mine = (y, x)

    def prepare(i):
        low, up = (first_lower, first_upper) if i == 0 else (rest_lower, rest_upper)
        offset = 0 if i == 0 else first
        for slot in range(2):
            live = slot < count[0]
            lo, uo = lower_list[0, slot], upper_list[0, slot]
            for g in range(CHUNKS[i] // GROUP):
                row = starts[i] + g * GROUP
                rows = pl.ds(row - offset, GROUP)
                moved = jnp.dot(place, low[lo, rows, :], preferred_element_type=jnp.float32)
                moved = jnp.where(live, moved, 0.0)
                lower_all[y, slot, pl.ds(row, GROUP), :] = moved.astype(jnp.bfloat16)
                upper_all[x, slot, pl.ds(row, GROUP), :] = up[uo, rows, :]

    def own(axis, way, i, origin):
        step = 1 - 2 * way
        part = buffers[axis].at[origin, :, pl.ds(starts[i], CHUNKS[i]), :]
        return pltpu.make_async_remote_copy(
            part, part, own_send.at[axis, way, i], own_recv.at[axis, way, i],
            device_id=at_ring(axis, step), device_id_type=MESH,
        )

    def fwd(axis, way, i, origin):
        step = 1 - 2 * way
        part = buffers[axis].at[origin, way, pl.ds(starts[i], CHUNKS[i]), :]
        return pltpu.make_async_remote_copy(
            part, part, fwd_send.at[axis, way, i], fwd_recv.at[axis, way, i],
            device_id=at_ring(axis, step), device_id_type=MESH,
        )

    links = [(axis, way) for way in (0, 1) for axis in (0, 1)]

    def send_own(i):
        for axis, way in links:
            own(axis, way, i, mine[axis]).start()

    def pass_on(i):
        for axis, way in links:
            origin = lax.rem(mine[axis] - (1 - 2 * way) + 4, 4)
            own(axis, way, i, origin).wait_recv()
            fwd(axis, way, i, origin).start()

    def wait_far(i):
        for axis, way in links:
            fwd(axis, way, i, lax.rem(mine[axis] + 2, 4)).wait_recv()

    far = lax.rem(y + 2, 4)
    apart = lax.rem(x - y + 4, 4)
    half = lax.div(apart, 2)
    near_js = (lax.rem(far + 2 - half, 4), lax.rem(far + 3 - lax.div(apart, 3), 4))
    far_js = (far, lax.rem(far + jnp.maximum(apart, 1), 4))
    all_js = (0, 1, 2, 3)

    def block(row, rows, col, cols, js, more, keep):
        total = None
        for j in js:
            for slot in range(2):
                term = lax.dot_general(
                    lower_all[j, slot, pl.ds(row, rows), :], upper_all[j, slot, pl.ds(col, cols), :],
                    NT, preferred_element_type=jnp.float32,
                )
                total = term if total is None else total + term
        into, row0, col0 = keep
        for g in range(rows // GROUP):
            at = (slice(None), slice(None), pl.ds((row - row0) // 16 + g * 8, 8), pl.ds(col - col0, cols))
            piece = total[g * GROUP : (g + 1) * GROUP].reshape(2, 8, 8, cols)
            into[at] = into[at] + piece if more else piece

    def cut(end):
        return [(r, min(256, end - r)) for r in range(0, end, 256)]

    def multiply(i, js, more, done):
        begin, end = edges[i], edges[i + 1]
        for row, rows in cut(end):
            block(row, rows, begin, end - begin, js, more, (product[i][0], 0, begin))
        if done:
            to_core(i, 0).start()
            pending.append([i, 0, 0])
        for col, cols in cut(begin):
            block(begin, end - begin, col, cols, js, more, (product[i][1], begin, 0))
        if done and i:
            to_core(i, 1).start()
            pending.append([i, 1, 0])

    def rect(i, k):
        begin, end = edges[i], edges[i + 1]
        if k == 0:
            return pl.ds(0, end // 16), pl.ds(begin, end - begin)
        return pl.ds(begin // 16, (end - begin) // 16), pl.ds(0, begin)

    def to_core(i, k):
        return pltpu.make_async_remote_copy(
            product[i][k].at[1 - core], from_core[i][k],
            core_send.at[i, k], core_recv.at[i, k],
            device_id={"layer": layer + sign}, device_id_type=MESH,
        )

    def to_z(i, k, slot, target, hop):
        return pltpu.make_async_remote_copy(
            product[i][k].at[core, lax.rem(z + target + 16, 8)], from_z[i][k].at[slot],
            z_send.at[i, k, slot], z_recv.at[i, k, slot],
            device_id=at_z(hop), device_id_type=MESH,
        )

    def parts(i):
        return (0, 1) if i else (0,)

    def add_core(i, k):
        to_core(i, k).wait_recv()

        @pl.loop(0, 8)
        def _(t):
            product[i][k][core, t] = product[i][k][core, t] + from_core[i][k][t]

    def add_z(i, k, slot, target):
        at = lax.rem(z + target + 16, 8)
        product[i][k][core, at] = product[i][k][core, at] + from_z[i][k][slot]

    def advance(i, k, step):
        if step == 0:
            add_core(i, k)
        if step:
            to_z(i, k, step - 1, 0, sign).wait_recv()
            add_z(i, k, step - 1, sign * (4 - step))
        if step < 4:
            to_z(i, k, step, sign * (4 - step), sign).start()
        if 0 < step < 4:
            to_z(i, k, 3 + step, 0, -sign).wait_recv()
            add_z(i, k, 3 + step, -sign * (3 - step))
        if step < 3:
            to_z(i, k, 4 + step, -sign * (3 - step), -sign).start()

    pending = []

    def tick():
        for entry in list(pending):
            advance(*entry)
            entry[2] += 1
            if entry[2] == STEPS:
                pending.remove(entry)

    loads[0].wait()
    loads[2].wait()
    prepare(0)
    pl.semaphore_wait(barrier, len(met))
    send_own(0)
    loads[1].wait()
    loads[3].wait()
    for i in range(1, AHEAD):
        prepare(i)
        send_own(i)
    for i in range(last + 1):
        if i + AHEAD <= last:
            prepare(i + AHEAD)
            send_own(i + AHEAD)
        pass_on(i)
        tick()
        near = [s for s, end in enumerate(ends) if end == i + 1 and SPLIT[s]]
        for strip in near:
            multiply(strip, near_js, False, False)
            tick()
        if i:
            wait_far(i - 1)
            tick()
        for strip, end in enumerate(ends):
            if end == i:
                multiply(strip, far_js if SPLIT[strip] else all_js, SPLIT[strip], True)
    wait_far(last)
    tick()
    multiply(len(STRIPS) - 1, far_js if SPLIT[-1] else all_js, SPLIT[-1], True)
    while pending:
        tick()

    for i in range(len(STRIPS)):
        for k in parts(i):
            rows, cols = rect(i, k)
            out[rows, cols] = product[i][k][core, z]

    for i in range(last + 1):
        for axis, way in links:
            own(axis, way, i, mine[axis]).wait_send()
            fwd(axis, way, i, lax.rem(mine[axis] - (1 - 2 * way) + 4, 4)).wait_send()
    for i in range(len(STRIPS)):
        for k in parts(i):
            to_core(i, k).wait_send()
            for slot in range(7):
                if slot < 4:
                    to_z(i, k, slot, sign * (4 - slot), sign).wait_send()
                else:
                    to_z(i, k, slot, -sign * (7 - slot), -sign).wait_send()


def per_device(
    lower_panels, upper_panels, lower_lists, upper_lists, block_counts, ancestor, pivot_inverse
):
    pool, rows, width = lower_panels.shape
    groups, _, cols = ancestor.shape
    chunks, strips = len(CHUNKS), len(STRIPS)
    smem = pl.BlockSpec(memory_space=pltpu.SMEM)
    vmem = pl.BlockSpec(memory_space=pltpu.VMEM)
    hbm = pl.BlockSpec(memory_space=pl.ANY)
    dma = pltpu.SemaphoreType.DMA

    def pieces(lead):
        shapes, begin = [], 0
        for i, count in enumerate(STRIPS):
            end = begin + sum(CHUNKS[sum(STRIPS[:i]) : sum(STRIPS[: i + 1])])
            down = pltpu.VMEM((*lead, end // 16, end - begin), jnp.float32)
            across = pltpu.VMEM((*lead, (end - begin) // 16, max(begin, 128)), jnp.float32)
            shapes.append((down, across) if begin else (down,))
            begin = end
        return tuple(shapes)

    total = pl.pallas_call(
        kernel,
        out_shape=jax.ShapeDtypeStruct((groups, cols), jnp.float32),
        in_specs=[smem, smem, smem, hbm, hbm],
        out_specs=vmem,
        scratch_shapes=[
            pltpu.VMEM((pool, CHUNKS[0], width), jnp.bfloat16),
            pltpu.VMEM((pool, CHUNKS[0], width), jnp.bfloat16),
            pltpu.VMEM((pool, rows - CHUNKS[0], width), jnp.bfloat16),
            pltpu.VMEM((pool, rows - CHUNKS[0], width), jnp.bfloat16),
            pltpu.VMEM((4, 2, rows, width), jnp.bfloat16),
            pltpu.VMEM((4, 2, cols, width), jnp.bfloat16),
            pieces((2, 8)),
            pieces((8,)),
            pieces((7,)),
            dma((2, 2)),
            dma((2, 2, chunks)),
            dma((2, 2, chunks)),
            dma((2, 2, chunks)),
            dma((2, 2, chunks)),
            dma((strips, 2)),
            dma((strips, 2)),
            dma((strips, 2, 7)),
            dma((strips, 2, 7)),
        ],
        compiler_params=pltpu.CompilerParams(
            collective_id=0, has_side_effects=True, vmem_limit_bytes=58 * 2**20
        ),
        cost_estimate=pl.CostEstimate(
            flops=4 * rows * cols * width * 4, bytes_accessed=9 * 2**20, transcendentals=0
        ),
    )(
        lower_lists, upper_lists, block_counts, lower_panels, upper_panels,
    )
    return (ancestor.astype(jnp.float32) - total.reshape(groups, 1, cols)) * pivot_inverse[:, :, None]


def solution(mesh):
    in_specs = (
        P("layer", "row", "col"),
        P("layer", "col", "row"),
        P("layer", None),
        P("layer", None),
        P("layer"),
        P("row", "layer", "col"),
        P("row", "layer"),
    )
    return jax.shard_map(
        per_device, mesh=mesh, in_specs=in_specs, out_specs=P("row", "layer", "col"), check_vma=False
    )
```
